512 devices in a mesh: height: 32 (over y_hi, x, core), chan: 16 (over y_lo, z).
Axes of the slice: x: 4, y: 8 (y_hi: 4, y_lo: 2; y = y_hi * 2 + y_lo), z: 8, core: 2. Of those that a mesh axis runs over, the one named last changes fastest.
Arguments:
- saved: int32 [4, 128, 120, 512], P(None, 'height', None, 'chan'), may hold values from -127 to 127
- exponents: int32 [4, 128, 120, 4], P(None, 'height'), may hold values from -14 to -10
- out_grad: bfloat16 [4, 128, 120, 512], P(None, 'height', None, 'chan'), may hold values from -6 to 6
- kernel: bfloat16 [512, 3, 3, 3, 512], P('chan', None, None, None, 'height'), may hold values from -0.0546875 to 0.0546875
Outputs:
- input_grad: bfloat16 [4, 128, 120, 512], P(None, 'height', None, 'chan')
- kernel_grad: float32 [512, 3, 3, 3, 512], P('chan', None, None, None, 'height')
The draws below stay inside these ranges and needn't reach their ends.
All inputs are finite; a program needn't handle non-finite values.
Results may differ from the reference program's by a relative error of at most 0.001.
Values may be sent and summed in bfloat16 or wider, within the bound.
No kernel may reach another device: no remote copies, remote signals or barrier semaphores. Data moves between devices by JAX's collectives and lax.ppermute only.
A program may use at most 192 MiB of HBM per device.

```python
import jax
import jax.numpy as jnp
from jax import lax

C = 512
QB = 128
TF = 4
W = 120
H = 128


def with_ends(array, stream_key, low, top_value):
    dims = array.shape
    place = [jax.random.randint(jax.random.fold_in(stream_key, axis), (), 0, dims[axis]) for axis in range(len(dims))]
    array = array.at[tuple(place)].set(low)
    longest = dims.index(max(dims))
    place[longest] = (place[longest] + 1) % dims[longest]
    return array.at[tuple(place)].set(top_value)


def steps_of(key, shape, split, low, top_value):
    def one(axis_at, blocks):
        draws = jax.random.uniform(jax.random.fold_in(jax.random.fold_in(key, 6), axis_at), (blocks,), jnp.float32, low / len(split), top_value / len(split))
        return jnp.repeat(jnp.exp(draws), shape[axis_at] // blocks).reshape((-1,) + (1,) * (len(shape) - axis_at - 1))

    level = one(*split[0])
    for cut in split[1:]:
        level = level * one(*cut)
    return level


def gaussian(own_key, dims, scale, bound, split=(), kind=jnp.bfloat16):
    array = jax.random.normal(own_key, dims, jnp.float32) * scale
    if len(split) > 0:
        array = steps_of(own_key, dims, split, -0.22, 0.18) * array
    return jnp.clip(array, min=-bound, max=bound).astype(kind)


def setup_inputs(seed: int = 0) -> dict:
    keys = jax.random.split(jax.random.key(seed), 5)
    return {
        "saved": with_ends(jax.random.randint(keys[0], (TF, H, W, C), -127, 128), jax.random.fold_in(keys[0], 1), -127, 127).astype(jnp.int32),
        "exponents": with_ends(jax.random.randint(keys[1], (TF, H, W, C // QB), -14, -9), jax.random.fold_in(keys[1], 1), -14, (-9) - 1).astype(jnp.int32),
        "out_grad": gaussian(keys[2], (TF, H, W, C), 1.0, 6.0, ((1, 32), (3, 16))),
        "kernel": gaussian(keys[3], (C, 3, 3, 3, C), (27 * C) ** -0.5, 0.0546875, ((0, 16), (4, 32))),
    }


def reference(saved, exponents, out_grad, kernel):
    factor = jnp.repeat(jnp.exp2(exponents.astype(jnp.float32)), QB, axis=3)
    rounded = (saved.astype(jnp.float32) * factor).astype(jnp.bfloat16)
    rounded = lax.optimization_barrier(rounded)
    inputs = rounded.astype(jnp.float32)
    frames, height, width, chans = out_grad.shape
    padded = jnp.pad(out_grad.astype(jnp.float32), ((0, 2), (1, 1), (1, 1), (0, 0)))
    x_rows = inputs.reshape(-1, chans)
    kernel_wide = kernel.astype(jnp.float32)
    input_sum = jnp.zeros((frames * height * width, chans), jnp.float32)
    blocks = []
    for frame_tap in range(3):
        for row_tap in range(3):
            for col_tap in range(3):
                shifted = padded[2 - frame_tap:2 - frame_tap + frames, 2 - row_tap:2 - row_tap + height, 2 - col_tap:2 - col_tap + width]
                shifted = shifted.reshape(-1, chans)
                input_sum = input_sum + jnp.dot(shifted, kernel_wide[:, frame_tap, row_tap, col_tap, :].T, preferred_element_type=jnp.float32)
                blocks.append(jnp.dot(x_rows.T, shifted, preferred_element_type=jnp.float32))
    kernel_grad = jnp.stack(blocks, axis=1).reshape(chans, 3, 3, 3, chans)
    input_grad = input_sum.reshape(frames, height, width, chans).astype(jnp.bfloat16)
    return input_grad, kernel_grad
```

```python
import jax
import jax.numpy as jnp
from jax import lax
from jax.experimental import pallas as pl
from jax.experimental.pallas import tpu as pltpu
from jax.sharding import Mesh, PartitionSpec as P

QB = 128
TAPS = 27
LANES = 128
COLS = 896
VMEM = 40 * 1024 * 1024
HEIGHT = ("a", "q", "c")
CHAN = ("b", "z")
f32 = jnp.float32
bf16 = jnp.bfloat16
f16 = jnp.float16
NT = (((1,), (1,)), ((), ()))


def call(body, out, scratch, flops, name, n_smem, n_in):
    smem = [pl.BlockSpec(memory_space=pltpu.SMEM)] * n_smem
    vmem = [pl.BlockSpec(memory_space=pltpu.VMEM)] * n_in
    outs = jax.tree.map(lambda _: pl.BlockSpec(memory_space=pltpu.VMEM), out)
    return pl.pallas_call(
        body,
        out_shape=out,
        in_specs=smem + vmem,
        out_specs=outs,
        scratch_shapes=scratch,
        compiler_params=pltpu.CompilerParams(vmem_limit_bytes=VMEM),
        cost_estimate=pl.CostEstimate(flops=flops, bytes_accessed=8000000, transcendentals=0),
        name=name,
    )


def frame_of(g_ref, t):
    blocks, _, rows, width, lanes = g_ref.shape
    return jnp.concatenate([g_ref[:, t, h].reshape(blocks * width, lanes) for h in range(rows)], axis=1)


def kernel_grad_body(where_ref, own_ref, other_ref, g_ref, keep_ref, send_ref, cols_ref, shifted_ref, acc_ref):
    half, core = where_ref[0], where_ref[1]
    frames, tall = own_ref.shape[:2]
    rows = tall - 2
    blocks = g_ref.shape[0]
    for ref, at in ((own_ref, half), (other_ref, 1 - half)):
        for s in range(frames):
            for r in range(tall):
                x = ref[s, r].astype(f32)
                cols_ref[0, s, r, at] = pltpu.roll(x, 1, 1).astype(bf16)
                cols_ref[1, s, r, at] = ref[s, r]
                cols_ref[2, s, r, at] = pltpu.roll(x, LANES - 1, 1).astype(bf16)
    shifted_ref[...] = jnp.zeros_like(shifted_ref)
    for t in range(frames):
        for tap in range(TAPS):
            a, b, c = tap // 9, tap // 3 % 3, tap % 3
            s = t - 2 + a
            if s < 0:
                continue
            for k in range(2):
                for h in range(rows):
                    shifted_ref[k * COLS + tap * 32:k * COLS + tap * 32 + 32, h * LANES:(h + 1) * LANES] = cols_ref[c, s, h + b, k]
        term = lax.dot_general(frame_of(g_ref, t), shifted_ref[...], NT, preferred_element_type=f32)
        term = term.reshape(blocks, 2, 16, 2 * COLS)
        if t == 0:
            acc_ref[...] = term
        else:
            acc_ref[...] += term
    for k in range(2):
        for q in range(blocks):
            keep_ref[k, q] = acc_ref[q, core, :, k * COLS:(k + 1) * COLS]
            send_ref[k, q] = acc_ref[q, 1 - core, :, k * COLS:(k + 1) * COLS]


def narrow_body(keep_ref, recv_ref, out_ref):
    total = keep_ref[...] + recv_ref[...]
    top = jnp.maximum(jnp.max(jnp.abs(total), keepdims=True), 2.0 ** -110)
    power = 14.0 - jnp.floor(jnp.log2(top))
    scaled = total * jnp.exp2(power)
    lane = lax.broadcasted_iota(jnp.int32, total.shape, len(total.shape) - 1)
    out = jnp.where(lane < TAPS * 32, scaled, power)
    out_ref[...] = out.reshape(out_ref.shape)


def widened(parts):
    parts = parts.astype(f32)
    return jnp.sum(parts * jnp.exp2(-parts[:, :, TAPS * 32:TAPS * 32 + 1]), axis=0)


def input_grad_body(where_ref, own_ref, other_ref, g_ref, keep_ref, send_ref, wide_ref, mats_ref, acc_ref):
    half, core = where_ref[0], where_ref[1]
    blocks, frames, rows = g_ref.shape[:3]
    for k in range(2):
        for q in range(blocks):
            wide_ref[k, q, core] = own_ref[k * blocks + q]
            wide_ref[k, q, 1 - core] = other_ref[k * blocks + q]
    for k in range(2):
        flat = wide_ref[k].reshape(blocks * 32, COLS).T
        for ab in range(9):
            mats_ref[ab, k * 96:k * 96 + 96] = flat[ab * 96:ab * 96 + 96]
    for s in range(frames):
        acc_ref[...] = jnp.zeros_like(acc_ref)
        for b in range(3):
            term = None
            for a in range(3):
                t = s + 2 - a
                if t >= frames:
                    continue
                one = jnp.dot(mats_ref[a * 3 + b], frame_of(g_ref, t), preferred_element_type=f32)
                term = one if term is None else term + one
            acc_ref[:, b * LANES:(b + rows) * LANES] += term
        for r in range(rows + 2):
            at = slice(r * LANES, (r + 1) * LANES)
            done = []
            for k in range(2):
                left = acc_ref[k * 96:k * 96 + 32, at]
                mid = acc_ref[k * 96 + 32:k * 96 + 64, at]
                right = acc_ref[k * 96 + 64:k * 96 + 96, at]
                done.append(mid + pltpu.roll(left, LANES - 1, 1) + pltpu.roll(right, 1, 1))
            first = half == 0
            keep_ref[s, r] = jnp.where(first, done[0], done[1])
            send_ref[s, r] = jnp.where(first, done[1], done[0])


def swap(axis, array):
    return lax.ppermute(array, axis, [(0, 1), (1, 0)])


def cross(array):
    return lax.ppermute(array, ("a", "b"), [(0, 0), (1, 2), (2, 1), (3, 3)])


def to_next(array):
    size = lax.axis_size(HEIGHT)
    return lax.ppermute(array, HEIGHT, [(i, i + 1) for i in range(size - 1)])


def to_prev(array):
    size = lax.axis_size(HEIGHT)
    return lax.ppermute(array, HEIGHT, [(i + 1, i) for i in range(size - 1)])


def lanes_padded(array):
    return jnp.pad(array, [(0, 0)] * (array.ndim - 1) + [(0, LANES - array.shape[-1])])


def local(saved, exponents, out_grad, kernel):
    frames, rows, width, ch = saved.shape
    zs = lax.axis_size("z")
    heights = lax.axis_size(("a", "q"))
    where = jnp.stack([lax.axis_index("b"), lax.axis_index("c")]).astype(jnp.int32)

    g_own = lanes_padded(out_grad.transpose(0, 1, 3, 2))
    g_all = lax.all_to_all(jnp.broadcast_to(g_own[None], (zs,) + g_own.shape), "z", 0, 0)

    first = lax.axis_index(CHAN) * ch // QB
    power = lax.dynamic_slice_in_dim(exponents.transpose(0, 1, 3, 2), first, 1, 2)
    x = saved.transpose(0, 1, 3, 2).astype(f32) * jnp.exp2(power.astype(f32))
    x = lanes_padded(x.astype(bf16))
    before, after = to_next(x[:, rows - 1:]), to_prev(x[:, :1])
    x_own = jnp.concatenate([before, x, after], axis=1)
    x_other = swap("b", x_own)

    flat = kernel.reshape(ch, TAPS, 16).transpose(2, 1, 0).reshape(16, TAPS * ch)
    flat = cross(jnp.pad(flat, ((0, 0), (0, COLS - TAPS * ch))))
    k_own = lax.all_to_all(jnp.broadcast_to(flat[None], (heights, 16, COLS)), ("a", "q"), 0, 0)
    k_other = swap("c", k_own)

    part = jax.ShapeDtypeStruct((2, zs, 16, COLS), f32)
    keep, send = call(
        kernel_grad_body,
        [part, part],
        [
            pltpu.VMEM((3, frames, rows + 2, 2, ch, LANES), bf16),
            pltpu.VMEM((2 * COLS, rows * LANES), bf16),
            pltpu.VMEM((zs, 2, 16, 2 * COLS), f32),
        ],
        2 * 2 * COLS * zs * 32 * frames * rows * LANES,
        "kernel_grad",
        1,
        3,
    )(where, x_own, x_other, g_all)
    parts = call(narrow_body, jax.ShapeDtypeStruct((heights, 16, COLS), f32), [], 1000000, "narrow", 0, 2)(keep, swap("c", send))
    parts = lax.all_to_all(parts.astype(f16), ("a", "q"), 0, 0)
    total = cross(widened(parts))[:, :TAPS * ch].reshape(16, TAPS, ch)
    kernel_grad = total.transpose(2, 1, 0).reshape(ch, 3, 3, 3, 16)

    grown = jax.ShapeDtypeStruct((frames, rows + 2, ch, LANES), f32)
    keep, send = call(
        input_grad_body,
        [grown, grown],
        [
            pltpu.VMEM((2, zs, 2, 16, COLS), bf16),
            pltpu.VMEM((9, 192, zs * 32), bf16),
            pltpu.VMEM((192, (rows + 2) * LANES), f32),
        ],
        2 * TAPS * 64 * zs * 32 * frames * rows * LANES,
        "input_grad",
        1,
        3,
    )(where, k_own, k_other, g_all)
    grown = keep + swap("b", send)
    above, below = to_next(grown[:, rows + 1]), to_prev(grown[:, 0])
    grad = grown[:, 1:rows + 1].at[:, 0].add(above).at[:, rows - 1].add(below)
    grad = grad[..., :width].astype(bf16).transpose(0, 1, 3, 2)
    return grad, kernel_grad


def solution(mesh):
    zs = mesh.shape["chan"] // 2
    fine = Mesh(mesh.devices.reshape(2, zs, 2, 2, zs), ("a", "q", "c", "b", "z"))
    in_specs = (
        P(None, HEIGHT, None, CHAN),
        P(None, HEIGHT, None, None),
        P(None, HEIGHT, None, CHAN),
        P(CHAN, None, None, None, HEIGHT),
    )
    out_specs = (P(None, HEIGHT, None, CHAN), P(CHAN, None, None, None, HEIGHT))
    return jax.shard_map(local, mesh=fine, in_specs=in_specs, out_specs=out_specs, check_vma=False)
```

```python
import jax
import jax.numpy as jnp
from jax import lax
from jax.experimental import pallas as pl
from jax.experimental.pallas import tpu as pltpu
from jax.sharding import Mesh, PartitionSpec as P

QB = 128
TAPS = 27
LANES = 128
COLS = 896
VMEM = 40 * 1024 * 1024
HEIGHT = ("a", "q", "c")
CHAN = ("b", "z")
f32 = jnp.float32
bf16 = jnp.bfloat16
f16 = jnp.float16
NT = (((1,), (1,)), ((), ()))


def call(body, out, scratch, flops, name, n_smem, n_in):
    smem = [pl.BlockSpec(memory_space=pltpu.SMEM)] * n_smem
    vmem = [pl.BlockSpec(memory_space=pltpu.VMEM)] * n_in
    outs = jax.tree.map(lambda _: pl.BlockSpec(memory_space=pltpu.VMEM), out)
    return pl.pallas_call(
        body,
        out_shape=out,
        in_specs=smem + vmem,
        out_specs=outs,
        scratch_shapes=scratch,
        compiler_params=pltpu.CompilerParams(vmem_limit_bytes=VMEM),
        cost_estimate=pl.CostEstimate(flops=flops, bytes_accessed=8000000, transcendentals=0),
        name=name,
    )


def frame_of(g_ref, t):
    blocks, _, rows, width, lanes = g_ref.shape
    return jnp.concatenate([g_ref[:, t, h].reshape(blocks * width, lanes) for h in range(rows)], axis=1)


def kernel_grad_body(where_ref, own_ref, other_ref, g_ref, keep_ref, send_ref, cols_ref, shifted_ref, acc_ref):
    half, core = where_ref[0], where_ref[1]
    frames, tall = own_ref.shape[:2]
    rows = tall - 2
    blocks = g_ref.shape[0]
    for ref, at in ((own_ref, half), (other_ref, 1 - half)):
        for s in range(frames):
            for r in range(tall):
                x = ref[s, r].astype(f32)
                cols_ref[0, s, r, at] = pltpu.roll(x, 1, 1).astype(bf16)
                cols_ref[1, s, r, at] = ref[s, r]
                cols_ref[2, s, r, at] = pltpu.roll(x, LANES - 1, 1).astype(bf16)
    shifted_ref[...] = jnp.zeros_like(shifted_ref)
    for t in range(frames):
        for tap in range(TAPS):
            a, b, c = tap // 9, tap // 3 % 3, tap % 3
            s = t - 2 + a
            if s < 0:
                continue
            for k in range(2):
                for h in range(rows):
                    shifted_ref[k * COLS + tap * 32:k * COLS + tap * 32 + 32, h * LANES:(h + 1) * LANES] = cols_ref[c, s, h + b, k]
        term = lax.dot_general(frame_of(g_ref, t), shifted_ref[...], NT, preferred_element_type=f32)
        term = term.reshape(blocks, 2, 16, 2 * COLS)
        if t == 0:
            acc_ref[...] = term
        else:
            acc_ref[...] += term
    for k in range(2):
        for q in range(blocks):
            keep_ref[k, q] = acc_ref[q, core, :, k * COLS:(k + 1) * COLS]
            send_ref[k, q] = acc_ref[q, 1 - core, :, k * COLS:(k + 1) * COLS]


def narrow_body(keep_ref, recv_ref, out_ref):
    total = keep_ref[...] + recv_ref[...]
    top = jnp.maximum(jnp.max(jnp.abs(total), keepdims=True), 2.0 ** -110)
    power = 14.0 - jnp.floor(jnp.log2(top))
    scaled = total * jnp.exp2(power)
    lane = lax.broadcasted_iota(jnp.int32, total.shape, len(total.shape) - 1)
    out = jnp.where(lane < TAPS * 32, scaled, power)
    out_ref[...] = out.reshape(out_ref.shape)


def widened(parts):
    parts = parts.astype(f32)
    return jnp.sum(parts * jnp.exp2(-parts[:, :, TAPS * 32:TAPS * 32 + 1]), axis=0)


def input_grad_body(where_ref, own_ref, other_ref, g_ref, keep_ref, send_ref, wide_ref, mats_ref, acc_ref):
    half, core, high, place = where_ref[0], where_ref[1], where_ref[2], where_ref[3]
    blocks, frames, rows = g_ref.shape[:3]
    for j, (k, q) in enumerate(gather_order(blocks)):
        wide_ref[high ^ k, place ^ q, core] = own_ref[j]
        wide_ref[high ^ k, place ^ q, 1 - core] = other_ref[j]
    for k in range(2):
        flat = wide_ref[k].reshape(blocks * 32, COLS).T
        for ab in range(9):
            mats_ref[ab, k * 96:k * 96 + 96] = flat[ab * 96:ab * 96 + 96]
    for s in range(frames):
        acc_ref[...] = jnp.zeros_like(acc_ref)
        for b in range(3):
            term = None
            for a in range(3):
                t = s + 2 - a
                if t >= frames:
                    continue
                one = jnp.dot(mats_ref[a * 3 + b], frame_of(g_ref, t), preferred_element_type=f32)
                term = one if term is None else term + one
            acc_ref[:, b * LANES:(b + rows) * LANES] += term
        for r in range(rows + 2):
            at = slice(r * LANES, (r + 1) * LANES)
            done = []
            for k in range(2):
                left = acc_ref[k * 96:k * 96 + 32, at]
                mid = acc_ref[k * 96 + 32:k * 96 + 64, at]
                right = acc_ref[k * 96 + 64:k * 96 + 96, at]
                done.append(mid + pltpu.roll(left, LANES - 1, 1) + pltpu.roll(right, 1, 1))
            first = half == 0
            keep_ref[s, r] = jnp.where(first, done[0], done[1])
            send_ref[s, r] = jnp.where(first, done[1], done[0])


def swap(axis, array):
    return lax.ppermute(array, axis, [(0, 1), (1, 0)])


def cross(array):
    return lax.ppermute(array, ("a", "b"), [(0, 0), (1, 2), (2, 1), (3, 3)])


def cross_other(array):
    return lax.ppermute(array, ("a", "b"), [(0, 2), (1, 0), (2, 3), (3, 1)])


def strides(size):
    return [1 << bit for bit in reversed(range(size.bit_length() - 1))]


def gather_order(size):
    order = [(0, 0), (1, 0)]
    for stride in strides(size):
        order = order + [(k, q | stride) for k, q in order]
    return order


def gathered(array):
    size = lax.axis_size("q")
    array = jnp.stack([cross(array), cross_other(array)])
    for stride in strides(size):
        other = lax.ppermute(array, "q", [(i, i ^ stride) for i in range(size)])
        array = jnp.concatenate([array, other])
    return array


def to_next(array):
    size = lax.axis_size(HEIGHT)
    return lax.ppermute(array, HEIGHT, [(i, i + 1) for i in range(size - 1)])


def to_prev(array):
    size = lax.axis_size(HEIGHT)
    return lax.ppermute(array, HEIGHT, [(i + 1, i) for i in range(size - 1)])


def lanes_padded(array):
    return jnp.pad(array, [(0, 0)] * (array.ndim - 1) + [(0, LANES - array.shape[-1])])


def local(saved, exponents, out_grad, kernel):
    frames, rows, width, ch = saved.shape
    zs = lax.axis_size("z")
    heights = lax.axis_size(("a", "q"))
    where = jnp.stack([lax.axis_index(axis) for axis in "bcaq"]).astype(jnp.int32)

    g_own = lanes_padded(out_grad.transpose(0, 1, 3, 2))
    g_all = lax.all_to_all(jnp.broadcast_to(g_own[None], (zs,) + g_own.shape), "z", 0, 0)

    first = lax.axis_index(CHAN) * ch // QB
    power = lax.dynamic_slice_in_dim(exponents.transpose(0, 1, 3, 2), first, 1, 2)
    x = saved.transpose(0, 1, 3, 2).astype(f32) * jnp.exp2(power.astype(f32))
    x = lanes_padded(x.astype(bf16))
    before, after = to_next(x[:, rows - 1:]), to_prev(x[:, :1])
    x_own = jnp.concatenate([before, x, after], axis=1)
    x_other = swap("b", x_own)

    flat = kernel.reshape(ch, TAPS, 16).transpose(2, 1, 0).reshape(16, TAPS * ch)
    k_own = gathered(jnp.pad(flat, ((0, 0), (0, COLS - TAPS * ch))))
    k_other = swap("c", k_own)

    part = jax.ShapeDtypeStruct((2, zs, 16, COLS), f32)
    keep, send = call(
        kernel_grad_body,
        [part, part],
        [
            pltpu.VMEM((3, frames, rows + 2, 2, ch, LANES), bf16),
            pltpu.VMEM((2 * COLS, rows * LANES), bf16),
            pltpu.VMEM((zs, 2, 16, 2 * COLS), f32),
        ],
        2 * 2 * COLS * zs * 32 * frames * rows * LANES,
        "kernel_grad",
        1,
        3,
    )(where, x_own, x_other, g_all)
    parts = call(narrow_body, jax.ShapeDtypeStruct((heights, 16, COLS), f32), [], 1000000, "narrow", 0, 2)(keep, swap("c", send))
    parts = lax.all_to_all(parts.astype(f16), ("a", "q"), 0, 0)
    total = cross(widened(parts))[:, :TAPS * ch].reshape(16, TAPS, ch)
    kernel_grad = total.transpose(2, 1, 0).reshape(ch, 3, 3, 3, 16)

    grown = jax.ShapeDtypeStruct((frames, rows + 2, ch, LANES), f32)
    keep, send = call(
        input_grad_body,
        [grown, grown],
        [
            pltpu.VMEM((2, zs, 2, 16, COLS), bf16),
            pltpu.VMEM((9, 192, zs * 32), bf16),
            pltpu.VMEM((192, (rows + 2) * LANES), f32),
        ],
        2 * TAPS * 64 * zs * 32 * frames * rows * LANES,
        "input_grad",
        1,
        3,
    )(where, k_own, k_other, g_all)
    grown = keep + swap("b", send)
    above, below = to_next(grown[:, rows + 1]), to_prev(grown[:, 0])
    grad = grown[:, 1:rows + 1].at[:, 0].add(above).at[:, rows - 1].add(below)
    grad = grad[..., :width].astype(bf16).transpose(0, 1, 3, 2)
    return grad, kernel_grad


def solution(mesh):
    zs = mesh.shape["chan"] // 2
    fine = Mesh(mesh.devices.reshape(2, zs, 2, 2, zs), ("a", "q", "c", "b", "z"))
    in_specs = (
        P(None, HEIGHT, None, CHAN),
        P(None, HEIGHT, None, None),
        P(None, HEIGHT, None, CHAN),
        P(CHAN, None, None, None, HEIGHT),
    )
    out_specs = (P(None, HEIGHT, None, CHAN), P(CHAN, None, None, None, HEIGHT))
    return jax.shard_map(local, mesh=fine, in_specs=in_specs, out_specs=out_specs, check_vma=False)
```

```python
import jax
import jax.numpy as jnp
from jax import lax
from jax.experimental import pallas as pl
from jax.experimental.pallas import tpu as pltpu
from jax.sharding import Mesh, PartitionSpec as P

QB = 128
TAPS = 27
LANES = 128
COLS = 896
VMEM = 40 * 1024 * 1024
HEIGHT = ("a", "q", "c")
CHAN = ("b", "z")
f32 = jnp.float32
bf16 = jnp.bfloat16
f16 = jnp.float16
NT = (((1,), (1,)), ((), ()))


def call(body, out, scratch, flops, name, n_smem, n_in):
    smem = [pl.BlockSpec(memory_space=pltpu.SMEM)] * n_smem
    vmem = [pl.BlockSpec(memory_space=pltpu.VMEM)] * n_in
    outs = jax.tree.map(lambda _: pl.BlockSpec(memory_space=pltpu.VMEM), out)
    return pl.pallas_call(
        body,
        out_shape=out,
        in_specs=smem + vmem,
        out_specs=outs,
        scratch_shapes=scratch,
        compiler_params=pltpu.CompilerParams(vmem_limit_bytes=VMEM),
        cost_estimate=pl.CostEstimate(flops=flops, bytes_accessed=8000000, transcendentals=0),
        name=name,
    )


def frame_of(g_ref, t):
    blocks, _, rows, width, lanes = g_ref.shape
    return jnp.concatenate([g_ref[:, t, h].reshape(blocks * width, lanes) for h in range(rows)], axis=1)


def kernel_grad_body(where_ref, own_ref, other_ref, g_ref, keep_ref, send_ref, cols_ref, shifted_ref, acc_ref):
    half, core = where_ref[0], where_ref[1]
    frames, tall = own_ref.shape[:2]
    rows = tall - 2
    blocks = g_ref.shape[0]
    for ref, at in ((own_ref, half), (other_ref, 1 - half)):
        for s in range(frames):
            for r in range(tall):
                x = ref[s, r].astype(f32)
                cols_ref[0, s, r, at] = pltpu.roll(x, 1, 1).astype(bf16)
                cols_ref[1, s, r, at] = ref[s, r]
                cols_ref[2, s, r, at] = pltpu.roll(x, LANES - 1, 1).astype(bf16)
    for t in reversed(range(frames)):
        low = max(0, 2 - t) * 9
        start = low * 32 // LANES * LANES
        for k in range(2):
            for tap in range(start // 32, TAPS + 1):
                at = k * COLS + tap * 32
                if tap < low or tap == TAPS:
                    shifted_ref[at:at + 32] = jnp.zeros((32, rows * LANES), bf16)
                    continue
                a, b, c = tap // 9, tap // 3 % 3, tap % 3
                for h in range(rows):
                    shifted_ref[at:at + 32, h * LANES:(h + 1) * LANES] = cols_ref[c, t - 2 + a, h + b, k]
        g = frame_of(g_ref, t)
        for at, end in [(0, 2 * COLS)] if start == 0 else [(start, COLS), (COLS + start, 2 * COLS)]:
            term = lax.dot_general(g, shifted_ref[at:end], NT, preferred_element_type=f32)
            term = term.reshape(blocks, 2, 16, end - at)
            if t == frames - 1:
                acc_ref[...] = term
            else:
                acc_ref[:, :, :, at:end] += term
    for k in range(2):
        for q in range(blocks):
            keep_ref[k, q] = acc_ref[q, core, :, k * COLS:(k + 1) * COLS]
            send_ref[k, q] = acc_ref[q, 1 - core, :, k * COLS:(k + 1) * COLS]


def narrow_body(keep_ref, recv_ref, out_ref):
    total = keep_ref[...] + recv_ref[...]
    top = jnp.maximum(jnp.max(jnp.abs(total), keepdims=True), 2.0 ** -110)
    power = 14.0 - jnp.floor(jnp.log2(top))
    scaled = total * jnp.exp2(power)
    lane = lax.broadcasted_iota(jnp.int32, total.shape, len(total.shape) - 1)
    out = jnp.where(lane < TAPS * 32, scaled, power)
    out_ref[...] = out.reshape(out_ref.shape)


def widened(parts):
    parts = parts.astype(f32)
    return jnp.sum(parts * jnp.exp2(-parts[:, :, TAPS * 32:TAPS * 32 + 1]), axis=0)


def input_grad_body(where_ref, own_ref, other_ref, g_ref, keep_ref, send_ref, wide_ref, mats_ref, acc_ref):
    half, core, high, place = where_ref[0], where_ref[1], where_ref[2], where_ref[3]
    blocks, frames, rows = g_ref.shape[:3]
    for j, (k, q) in enumerate(gather_order(blocks)):
        wide_ref[high ^ k, place ^ q, core] = own_ref[j]
        wide_ref[high ^ k, place ^ q, 1 - core] = other_ref[j]
    for k in range(2):
        flat = wide_ref[k].reshape(blocks * 32, COLS).T
        for ab in range(9):
            mats_ref[ab, k * 96:k * 96 + 96] = flat[ab * 96:ab * 96 + 96]
    for s in range(frames):
        acc_ref[...] = jnp.zeros_like(acc_ref)
        for b in range(3):
            term = None
            for a in range(3):
                t = s + 2 - a
                if t >= frames:
                    continue
                one = jnp.dot(mats_ref[a * 3 + b], frame_of(g_ref, t), preferred_element_type=f32)
                term = one if term is None else term + one
            acc_ref[:, b * LANES:(b + rows) * LANES] += term
        for r in range(rows + 2):
            at = slice(r * LANES, (r + 1) * LANES)
            done = []
            for k in range(2):
                left = acc_ref[k * 96:k * 96 + 32, at]
                mid = acc_ref[k * 96 + 32:k * 96 + 64, at]
                right = acc_ref[k * 96 + 64:k * 96 + 96, at]
                done.append(mid + pltpu.roll(left, LANES - 1, 1) + pltpu.roll(right, 1, 1))
            first = half == 0
            keep_ref[s, r] = jnp.where(first, done[0], done[1])
            send_ref[s, r] = jnp.where(first, done[1], done[0])


def swap(axis, array):
    return lax.ppermute(array, axis, [(0, 1), (1, 0)])


def cross(array):
    return lax.ppermute(array, ("a", "b"), [(0, 0), (1, 2), (2, 1), (3, 3)])


def cross_other(array):
    return lax.ppermute(array, ("a", "b"), [(0, 2), (1, 0), (2, 3), (3, 1)])


def strides(size):
    return [1 << bit for bit in reversed(range(size.bit_length() - 1))]


def gather_order(size):
    order = [(0, 0), (1, 0)]
    for stride in strides(size):
        order = order + [(k, q | stride) for k, q in order]
    return order


def gathered(array):
    size = lax.axis_size("q")
    array = jnp.stack([cross(array), cross_other(array)])
    for stride in strides(size):
        other = lax.ppermute(array, "q", [(i, i ^ stride) for i in range(size)])
        array = jnp.concatenate([array, other])
    return array


def to_next(array):
    size = lax.axis_size(HEIGHT)
    return lax.ppermute(array, HEIGHT, [(i, i + 1) for i in range(size - 1)])


def to_prev(array):
    size = lax.axis_size(HEIGHT)
    return lax.ppermute(array, HEIGHT, [(i + 1, i) for i in range(size - 1)])


def lanes_padded(array):
    return jnp.pad(array, [(0, 0)] * (array.ndim - 1) + [(0, LANES - array.shape[-1])])


def local(saved, exponents, out_grad, kernel):
    frames, rows, width, ch = saved.shape
    zs = lax.axis_size("z")
    heights = lax.axis_size(("a", "q"))
    where = jnp.stack([lax.axis_index(axis) for axis in "bcaq"]).astype(jnp.int32)

    g_own = lanes_padded(out_grad.transpose(0, 1, 3, 2))
    g_all = lax.all_to_all(jnp.broadcast_to(g_own[None], (zs,) + g_own.shape), "z", 0, 0)

    first = lax.axis_index(CHAN) * ch // QB
    power = lax.dynamic_slice_in_dim(exponents.transpose(0, 1, 3, 2), first, 1, 2)
    x = saved.transpose(0, 1, 3, 2).astype(f32) * jnp.exp2(power.astype(f32))
    x = lanes_padded(x.astype(bf16))
    before, after = to_next(x[:, rows - 1:]), to_prev(x[:, :1])
    x_own = jnp.concatenate([before, x, after], axis=1)
    x_other = swap("b", x_own)

    flat = kernel.reshape(ch, TAPS, 16).transpose(2, 1, 0).reshape(16, TAPS * ch)
    k_own = gathered(jnp.pad(flat, ((0, 0), (0, COLS - TAPS * ch))))
    k_other = swap("c", k_own)

    part = jax.ShapeDtypeStruct((2, zs, 16, COLS), f32)
    keep, send = call(
        kernel_grad_body,
        [part, part],
        [
            pltpu.VMEM((3, frames, rows + 2, 2, ch, LANES), bf16),
            pltpu.VMEM((2 * COLS, rows * LANES), bf16),
            pltpu.VMEM((zs, 2, 16, 2 * COLS), f32),
        ],
        2 * 2 * COLS * zs * 32 * frames * rows * LANES,
        "kernel_grad",
        1,
        3,
    )(where, x_own, x_other, g_all)
    parts = call(narrow_body, jax.ShapeDtypeStruct((heights, 16, COLS), f32), [], 1000000, "narrow", 0, 2)(keep, swap("c", send))
    parts = lax.all_to_all(parts.astype(f16), ("a", "q"), 0, 0)
    total = cross(widened(parts))[:, :TAPS * ch].reshape(16, TAPS, ch)
    kernel_grad = total.transpose(2, 1, 0).reshape(ch, 3, 3, 3, 16)

    grown = jax.ShapeDtypeStruct((frames, rows + 2, ch, LANES), f32)
    keep, send = call(
        input_grad_body,
        [grown, grown],
        [
            pltpu.VMEM((2, zs, 2, 16, COLS), bf16),
            pltpu.VMEM((9, 192, zs * 32), bf16),
            pltpu.VMEM((192, (rows + 2) * LANES), f32),
        ],
        2 * TAPS * 64 * zs * 32 * frames * rows * LANES,
        "input_grad",
        1,
        3,
    )(where, k_own, k_other, g_all)
    grown = keep + swap("b", send)
    above, below = to_next(grown[:, rows + 1]), to_prev(grown[:, 0])
    grad = grown[:, 1:rows + 1].at[:, 0].add(above).at[:, rows - 1].add(below)
    grad = grad[..., :width].astype(bf16).transpose(0, 1, 3, 2)
    return grad, kernel_grad


def solution(mesh):
    zs = mesh.shape["chan"] // 2
    fine = Mesh(mesh.devices.reshape(2, zs, 2, 2, zs), ("a", "q", "c", "b", "z"))
    in_specs = (
        P(None, HEIGHT, None, CHAN),
        P(None, HEIGHT, None, None),
        P(None, HEIGHT, None, CHAN),
        P(CHAN, None, None, None, HEIGHT),
    )
    out_specs = (P(None, HEIGHT, None, CHAN), P(CHAN, None, None, None, HEIGHT))
    return jax.shard_map(local, mesh=fine, in_specs=in_specs, out_specs=out_specs, check_vma=False)
```
